256 devices in a mesh: lon: 16 (over x_hi, y, core), lat: 16 (over z, x_lo).
Axes of the slice: x: 4 (x_hi: 2, x_lo: 2; x = x_hi * 2 + x_lo), y: 4, z: 8, core: 2. Of those that a mesh axis runs over, the one named last changes fastest.
Arguments:
- input_first_batch: bfloat16 [2, 192, 192, 1024], P(None, 'lat', 'lon'), may hold values from -6 to 6
- input_second_batch: bfloat16 [2, 192, 192, 1024], P(None, 'lat', 'lon'), may hold values from -6 to 6
- cotangent_second_batch: bfloat16 [2, 192, 192, 1024], P(None, 'lat', 'lon'), may hold values from -6 to 6
- layer_norm_gain: float32 [1024], replicated, may hold values from 0.1 to 1.9
- query_key_value_weight: bfloat16 [1024, 3072], replicated, may hold values from -2 to 2
- output_projection_weight: bfloat16 [1024, 1024], replicated, may hold values from -0.1875 to 0.1875
- projection_adapter_down: bfloat16 [1024, 8], replicated, may hold values from -0.1875 to 0.1875
- projection_adapter_up: bfloat16 [8, 3072], replicated, may hold values from -2 to 2
- output_adapter_down: bfloat16 [1024, 8], replicated, may hold values from -0.1875 to 0.1875
- output_adapter_up: bfloat16 [8, 1024], replicated, may hold values from -2 to 2
Outputs:
- output_a: bfloat16 [2, 192, 192, 1024], P(None, 'lat', 'lon')
- input_grad_b: bfloat16 [2, 192, 192, 1024], P(None, 'lat', 'lon')
- grad_qkv_down: float32 [1024, 8], replicated
- grad_qkv_up: float32 [8, 3072], replicated
- grad_out_down: float32 [1024, 8], replicated
- grad_out_up: float32 [8, 1024], replicated
The draws below stay inside these ranges and needn't reach their ends.
All inputs are finite; a program needn't handle non-finite values.
Results may differ from the reference program's by a relative error of at most 0.017.
Values may be sent and summed in bfloat16 or wider, within the bound.
No kernel may reach another device: no remote copies, remote signals or barrier semaphores. Data moves between devices by JAX's collectives and lax.ppermute only.
A program may use at most 128 MiB of HBM per device.

```python
import jax
import jax.numpy as jnp
from jax import lax

MODEL_WIDTH = 1024
HEAD_DIM = 64
ADAPTER_RANK = 8
LEV = 2
WIN_LAT = 12
WIN_LON = 6
NLAT = 192
NLON = 192
N_LAT = 16


def draw_query_key_value_weight(key, part):
    key = jax.random.fold_in(key, 11)
    base_key = jax.random.fold_in(key, 0)
    base = jax.random.normal(base_key, (MODEL_WIDTH, 3 * MODEL_WIDTH), jnp.float32) * MODEL_WIDTH ** (-0.5)
    return base.astype(jnp.bfloat16)


def block_levels(rng, dims, cuts, smallest, top_value):
    factor_of, own = 1.0, jax.random.fold_in(rng, 6)
    for dim, shards_of in cuts:
        draws = jnp.exp(jax.random.uniform(jax.random.fold_in(own, dim), (shards_of,), jnp.float32, smallest / len(cuts), top_value / len(cuts)))
        factor_of = factor_of * jnp.repeat(draws, dims[dim] // shards_of).reshape([-1 if axis == dim else 1 for axis in range(len(dims))])
    return factor_of


def normal_values(rng, dims, width, reach, shards=(), kind=jnp.bfloat16):
    factor_of = block_levels(rng, dims, shards, -0.22, 0.18) if shards else 1.0
    values = jax.random.normal(rng, dims, jnp.float32) * width * factor_of
    return jnp.minimum(jnp.maximum(values, -reach), reach).astype(kind)


def setup_inputs(seed: int = 0) -> dict:
    arg_keys = jax.random.split(jax.random.key(seed), 11)
    return {
        "input_first_batch": normal_values(arg_keys[0], (LEV, NLAT, NLON, MODEL_WIDTH), 1.0, 6.0, ((1, 16), (2, 16))),
        "input_second_batch": normal_values(arg_keys[1], (LEV, NLAT, NLON, MODEL_WIDTH), 1.0, 6.0, ((1, 16), (2, 16))),
        "cotangent_second_batch": normal_values(arg_keys[2], (LEV, NLAT, NLON, MODEL_WIDTH), 1.0, 6.0, ((1, 16), (2, 16))),
        "layer_norm_gain": jnp.clip(1.0 + 0.18 * jax.random.normal(arg_keys[3], (MODEL_WIDTH,), jnp.float32), 0.1, 1.9),
        "query_key_value_weight": draw_query_key_value_weight(jax.random.fold_in(arg_keys[10], 71), 0),
        "output_projection_weight": normal_values(arg_keys[5], (MODEL_WIDTH, MODEL_WIDTH), MODEL_WIDTH ** -0.5, 0.1875),
        "projection_adapter_down": normal_values(arg_keys[6], (MODEL_WIDTH, ADAPTER_RANK), MODEL_WIDTH ** -0.5, 0.1875),
        "projection_adapter_up": normal_values(arg_keys[7], (ADAPTER_RANK, 3 * MODEL_WIDTH), ADAPTER_RANK ** -0.5, 2.0),
        "output_adapter_down": normal_values(arg_keys[8], (MODEL_WIDTH, ADAPTER_RANK), MODEL_WIDTH ** -0.5, 0.1875),
        "output_adapter_up": normal_values(arg_keys[9], (ADAPTER_RANK, MODEL_WIDTH), ADAPTER_RANK ** -0.5, 2.0),
    }


epsilon = 1e-05
masked_score = -1e+30

def product_float32(left_op, right_op):
    return jnp.dot(left_op, right_op, preferred_element_type=jnp.float32)

def matmul_tn(left_op, right_op):
    return lax.dot_general(left_op, right_op, (((0,), (0,)), ((), ())), preferred_element_type=jnp.float32)

def product_transposed_right(left_op, right_op):
    return lax.dot_general(left_op, right_op, (((1,), (1,)), ((), ())), preferred_element_type=jnp.float32)

def to_windows(band_slab):
    lev_count, row_count, col_count, features = band_slab.shape
    blocks = band_slab.reshape(lev_count, row_count, col_count // WIN_LON, WIN_LON, features)
    blocks = jnp.transpose(blocks, (2, 0, 1, 3, 4))
    return blocks.reshape(col_count // WIN_LON, lev_count * row_count * WIN_LON, features)

def from_windows(windowed, lev_count, row_count):
    win_count, points, features = windowed.shape
    blocks = windowed.reshape(win_count, lev_count, row_count, WIN_LON, features)
    blocks = jnp.transpose(blocks, (1, 2, 0, 3, 4))
    return blocks.reshape(lev_count, row_count, win_count * WIN_LON, features)

def split_heads(projected_rows):
    win_count, points, _ = projected_rows.shape
    pieces = projected_rows.reshape(win_count, points, 3, MODEL_WIDTH // HEAD_DIM, HEAD_DIM)
    return (pieces[:, :, 0].astype(jnp.float32), pieces[:, :, 1].astype(jnp.float32), pieces[:, :, 2].astype(jnp.float32))

def attend(projected_rows, polar):
    win_count, points, _ = projected_rows.shape
    queries, key_part, values = split_heads(projected_rows)
    scores = jnp.einsum('wqhe,wkhe->whqk', queries, key_part) * HEAD_DIM ** (-0.5)
    row_index = jnp.arange(points) // WIN_LON % WIN_LAT
    upper_half = row_index < WIN_LAT // 2
    allowed = jnp.logical_or(upper_half[:, None] == upper_half[None, :], jnp.logical_not(polar))
    scores = jnp.where(allowed, scores, masked_score)
    softmaxed = jax.nn.softmax(scores, axis=-1)
    weights = softmaxed.astype(jnp.bfloat16)
    context = jnp.einsum('whqk,wkhe->wqhe', weights.astype(jnp.float32), values).astype(jnp.bfloat16)
    return (context.reshape(win_count, points, MODEL_WIDTH), softmaxed, weights)

def attend_back(context_gradient, projected_rows, softmaxed, weights):
    win_count, points, _ = projected_rows.shape
    queries, key_part, values = split_heads(projected_rows)
    grad_ctx = context_gradient.reshape(win_count, points, MODEL_WIDTH // HEAD_DIM, HEAD_DIM).astype(jnp.float32)
    grad_weights = jnp.einsum('wqhe,wkhe->whqk', grad_ctx, values)
    grad_values = jnp.einsum('whqk,wqhe->wkhe', weights.astype(jnp.float32), grad_ctx)
    inner = lax.optimization_barrier(jnp.sum(grad_weights * softmaxed, axis=-1, keepdims=True))
    grad_scores = (softmaxed * (grad_weights - inner) * HEAD_DIM ** (-0.5)).astype(jnp.bfloat16)
    grad_queries = jnp.einsum('whqk,wkhe->wqhe', grad_scores.astype(jnp.float32), key_part)
    grad_keys = jnp.einsum('whqk,wqhe->wkhe', grad_scores.astype(jnp.float32), queries)
    joined = jnp.stack([grad_queries, grad_keys, grad_values], axis=2)
    return joined.reshape(win_count, points, 3 * MODEL_WIDTH).astype(jnp.bfloat16)

def forward_band(band_slab, parameters, polar):
    layer_norm_gain, query_key_value_weight, output_projection_weight, projection_adapter_down, projection_adapter_up, output_adapter_down, output_adapter_up = parameters
    lev_count, row_count = (band_slab.shape[0], band_slab.shape[1])
    windowed = to_windows(band_slab)
    win_count, points = (windowed.shape[0], windowed.shape[1])
    tokens_in = windowed.reshape(win_count * points, MODEL_WIDTH).astype(jnp.float32)
    average = lax.optimization_barrier(jnp.mean(tokens_in, axis=-1, keepdims=True))
    centered = tokens_in - average
    variance = lax.optimization_barrier(jnp.mean(centered * centered, axis=-1, keepdims=True))
    inv_std = lax.rsqrt(variance + epsilon)
    standard = centered * inv_std
    normalized_input = (standard * layer_norm_gain).astype(jnp.bfloat16)
    adapter_projection_latent = product_float32(normalized_input, projection_adapter_down).astype(jnp.bfloat16)
    projected_rows = (product_float32(normalized_input, query_key_value_weight) + product_float32(adapter_projection_latent, projection_adapter_up)).astype(jnp.bfloat16)
    projected_rows = projected_rows.reshape(win_count, points, 3 * MODEL_WIDTH)
    context, softmaxed, weights = attend(projected_rows, polar)
    context_matrix = context.reshape(win_count * points, MODEL_WIDTH)
    adapter_output_latent = product_float32(context_matrix, output_adapter_down).astype(jnp.bfloat16)
    branch_output = (product_float32(context_matrix, output_projection_weight) + product_float32(adapter_output_latent, output_adapter_up)).astype(jnp.bfloat16)
    slab_out = from_windows(branch_output.reshape(win_count, points, MODEL_WIDTH), lev_count, row_count)
    return (slab_out, (standard, inv_std, normalized_input, adapter_projection_latent, projected_rows, softmaxed, weights, context_matrix, adapter_output_latent))

def backward_band(saved, cot_slab, parameters):
    layer_norm_gain, query_key_value_weight, output_projection_weight, projection_adapter_down, projection_adapter_up, output_adapter_down, output_adapter_up = parameters
    standard, inv_std, normalized_input, adapter_projection_latent, projected_rows, softmaxed, weights, context_matrix, adapter_output_latent = saved
    lev_count, row_count = (cot_slab.shape[0], cot_slab.shape[1])
    cot_win = to_windows(cot_slab)
    win_count, points = (cot_win.shape[0], cot_win.shape[1])
    cotangent_rows = cot_win.reshape(win_count * points, MODEL_WIDTH)
    raw_out_up = matmul_tn(adapter_output_latent, cotangent_rows)
    cotangent_adapter_output = product_transposed_right(cotangent_rows, output_adapter_up).astype(jnp.bfloat16)
    raw_out_down = matmul_tn(context_matrix, cotangent_adapter_output)
    context_gradient = (product_transposed_right(cotangent_rows, output_projection_weight) + product_transposed_right(cotangent_adapter_output, output_adapter_down)).astype(jnp.bfloat16)
    projected_gradient = attend_back(context_gradient.reshape(win_count, points, MODEL_WIDTH), projected_rows, softmaxed, weights)
    projected_gradient = projected_gradient.reshape(win_count * points, 3 * MODEL_WIDTH)
    raw_qkv_up = matmul_tn(adapter_projection_latent, projected_gradient)
    cotangent_adapter_projection = product_transposed_right(projected_gradient, projection_adapter_up).astype(jnp.bfloat16)
    raw_qkv_down = matmul_tn(normalized_input, cotangent_adapter_projection)
    normalized_gradient = product_transposed_right(projected_gradient, query_key_value_weight) + product_transposed_right(cotangent_adapter_projection, projection_adapter_down)
    grad_hat = normalized_gradient * layer_norm_gain
    grad_rows = inv_std * (grad_hat - lax.optimization_barrier(jnp.mean(grad_hat, axis=-1, keepdims=True)) - standard * lax.optimization_barrier(jnp.mean(grad_hat * standard, axis=-1, keepdims=True)))
    grad_slab = from_windows(grad_rows.astype(jnp.bfloat16).reshape(win_count, points, MODEL_WIDTH), lev_count, row_count)
    return (grad_slab, (raw_qkv_down, raw_qkv_up, raw_out_down, raw_out_up))

def reference(input_first_batch, input_second_batch, cotangent_second_batch, layer_norm_gain, query_key_value_weight, output_projection_weight, projection_adapter_down, projection_adapter_up, output_adapter_down, output_adapter_up):
    parameters = (layer_norm_gain, query_key_value_weight, output_projection_weight, projection_adapter_down, projection_adapter_up, output_adapter_down, output_adapter_up)
    half_rows = WIN_LAT // 2
    half_cols = WIN_LON // 2

    def to_bands(field_in):
        shifted = jnp.roll(field_in, (-half_rows, -half_cols), axis=(1, 2))
        return jnp.transpose(shifted.reshape(LEV, N_LAT, WIN_LAT, NLON, MODEL_WIDTH), (1, 0, 2, 3, 4))

    def from_bands(bands):
        field_out = jnp.transpose(bands, (1, 0, 2, 3, 4)).reshape(LEV, NLAT, NLON, MODEL_WIDTH)
        return jnp.roll(field_out, (half_rows, half_cols), axis=(1, 2))
    polar_flags = jnp.arange(N_LAT) == N_LAT - 1

    def forward_item(band_item):
        return forward_band(band_item[0], parameters, band_item[1])[0]
    branch_a = lax.map(forward_item, (to_bands(input_first_batch), polar_flags))
    output_a = (input_first_batch.astype(jnp.float32) + from_bands(branch_a).astype(jnp.float32)).astype(jnp.bfloat16)

    def step_band(sums_so_far, band_item):
        band_b, band_cot, polar = band_item
        _, saved = forward_band(band_b, parameters, polar)
        grad_slab, grad_terms = backward_band(saved, band_cot, parameters)
        return (jax.tree.map(jnp.add, sums_so_far, grad_terms), grad_slab)
    start_sums = (jnp.zeros((MODEL_WIDTH, ADAPTER_RANK), jnp.float32), jnp.zeros((ADAPTER_RANK, 3 * MODEL_WIDTH), jnp.float32), jnp.zeros((MODEL_WIDTH, ADAPTER_RANK), jnp.float32), jnp.zeros((ADAPTER_RANK, MODEL_WIDTH), jnp.float32))
    raw_grads, grad_bands = lax.scan(step_band, start_sums, (to_bands(input_second_batch), to_bands(cotangent_second_batch), polar_flags))
    input_grad_b = (cotangent_second_batch.astype(jnp.float32) + from_bands(grad_bands).astype(jnp.float32)).astype(jnp.bfloat16)
    raw_qkv_down, raw_qkv_up, raw_out_down, raw_out_up = raw_grads
    sq_total = jnp.sum(raw_qkv_down * raw_qkv_down) + jnp.sum(raw_qkv_up * raw_qkv_up) + jnp.sum(raw_out_down * raw_out_down) + jnp.sum(raw_out_up * raw_out_up)
    factor = jnp.minimum(1.0, jnp.sqrt(6.0 * MODEL_WIDTH * ADAPTER_RANK) / (jnp.sqrt(sq_total) + 1e-06))
    return (output_a, input_grad_b, raw_qkv_down * factor, raw_qkv_up * factor, raw_out_down * factor, raw_out_up * factor)
```

```python
import functools

import jax
import jax.numpy as jnp
from jax import lax
from jax.experimental import pallas as pl
from jax.experimental.pallas import tpu as pltpu
from jax.sharding import PartitionSpec as P

D = 1024
HD = 64
RANK = 8
TOK = 288
WIN = 144
HALF = 72
GH = 4
GW = GH * HD
NG = D // GW
GQ = GH * WIN
EPS = 1e-05
MASKED = -1e30
VMEM = 40 * 1024 * 1024
F32 = jnp.float32
BF16 = jnp.bfloat16


def nn(a, b):
    return jnp.dot(a, b, preferred_element_type=F32)


def nt(a, b):
    return lax.dot_general(a, b, (((1,), (1,)), ((), ())), preferred_element_type=F32)


def tn(a, b):
    return lax.dot_general(a, b, (((0,), (0,)), ((), ())), preferred_element_type=F32)


def layer_norm(tokens):
    average = jnp.mean(tokens, axis=-1, keepdims=True)
    centered = tokens - average
    variance = jnp.mean(centered * centered, axis=-1, keepdims=True)
    inv_std = lax.rsqrt(variance + EPS)
    return centered * inv_std, inv_std


def assemble(pieces, out_ref):
    at = 0
    for piece in pieces:
        rows = piece.shape[0]
        out_ref[at : at + rows] = piece[...].astype(F32)
        at += rows


def take_apart(rows_ref, pieces):
    at = 0
    for piece in pieces:
        rows = piece.shape[0]
        piece[...] = rows_ref[at : at + rows].astype(BF16)
        at += rows


def head_lanes(h):
    lane = lax.broadcasted_iota(jnp.int32, (1, GW), 1)
    return (lane >= h * HD) & (lane < (h + 1) * HD)


def spread_heads(a):
    zero = jnp.zeros_like(a)
    return jnp.concatenate([jnp.where(head_lanes(h), a, zero) for h in range(GH)], axis=0)


def gather_heads(a):
    out = a[:WIN]
    for h in range(1, GH):
        out = jnp.where(head_lanes(h), a[h * WIN : (h + 1) * WIN], out)
    return out


def pole_bias(polar):
    key = lax.broadcasted_iota(jnp.int32, (WIN, GQ), 0)
    query = lax.broadcasted_iota(jnp.int32, (WIN, GQ), 1)
    for h in range(1, GH):
        query = jnp.where(query >= WIN, query - WIN, query)
    apart = jnp.not_equal(key < HALF, query < HALF)
    return jnp.where(apart & (polar != 0), MASKED, 0.0)


def softmax_keys(q_blocks, k, bias_ref):
    scores = nt(k, q_blocks) + bias_ref[...]
    top = jnp.max(scores, axis=0, keepdims=True)
    p = jnp.exp(scores - top)
    return p * (1.0 / jnp.sum(p, axis=0, keepdims=True))


def project(normed, low, w_ref, up_ref, cols):
    return (nn(normed, w_ref[:, cols]) + nn(low, up_ref[:, cols])).astype(BF16)


def columns(i, g):
    return slice(i * D + g * GW, i * D + (g + 1) * GW)


def forward_kernel(
    polar_ref, x0, x1, x2, x3, x4, gain_ref, wqkv_ref, wo_ref, pd_ref, pu_ref, od_ref, ou_ref,
    o0, o1, o2, o3, o4, x_ref, bias_ref,
):
    assemble((x0, x1, x2, x3, x4), x_ref)
    standard, _ = layer_norm(x_ref[...])
    normed = (standard * gain_ref[...]).astype(BF16)
    low = nt(normed, pd_ref[...]).astype(BF16)
    bias_ref[...] = pole_bias(polar_ref[0])
    groups = []
    for g in range(NG):
        q = project(normed, low, wqkv_ref, pu_ref, columns(0, g)) * 0.125
        k = project(normed, low, wqkv_ref, pu_ref, columns(1, g))
        v = project(normed, low, wqkv_ref, pu_ref, columns(2, g))
        contexts = []
        for w in range(2):
            rows = slice(w * WIN, (w + 1) * WIN)
            weights = softmax_keys(spread_heads(q[rows]), k[rows], bias_ref).astype(BF16)
            contexts.append(gather_heads(tn(weights, v[rows])).astype(BF16))
        groups.append(jnp.concatenate(contexts, axis=0))
    context = jnp.concatenate(groups, axis=1)
    low_out = nt(context, od_ref[...]).astype(BF16)
    x_ref[...] = nn(context, wo_ref[...]) + nn(low_out, ou_ref[...])
    take_apart(x_ref, (o0, o1, o2, o3, o4))


def grads_kernel(
    polar_ref, x0, x1, x2, x3, x4, c0, c1, c2, c3, c4, gain_ref, wqkv_ref, wo_ref, pd_ref, pu_ref,
    od_ref, ou_ref, x_ref, gp_ref, clq_ref, grads_ref, rows_ref, bias_ref,
):
    assemble((x0, x1, x2, x3, x4), x_ref)
    assemble((c0, c1, c2, c3, c4), rows_ref)
    cot = rows_ref[...].astype(BF16)
    standard, _ = layer_norm(x_ref[...])
    normed = (standard * gain_ref[...]).astype(BF16)
    low = nt(normed, pd_ref[...])
    lowt = low.T.astype(BF16)
    low = low.astype(BF16)
    clo = nt(cot, ou_ref[...])
    clot = clo.T.astype(BF16)
    clo = clo.astype(BF16)
    bias_ref[...] = pole_bias(polar_ref[0])
    low_out = jnp.zeros((TOK, RANK), F32)
    cl = jnp.zeros((TOK, RANK), F32)
    for g in range(NG):
        own = columns(0, g)
        q = project(normed, low, wqkv_ref, pu_ref, columns(0, g)) * 0.125
        k = project(normed, low, wqkv_ref, pu_ref, columns(1, g))
        v = project(normed, low, wqkv_ref, pu_ref, columns(2, g))
        grad_context = (nt(cot, wo_ref[own, :]) + nn(clo, od_ref[:, own])).astype(BF16)
        contexts, gqs, gks, gvs = [], [], [], []
        for w in range(2):
            rows = slice(w * WIN, (w + 1) * WIN)
            q_blocks, g_blocks = spread_heads(q[rows]), spread_heads(grad_context[rows])
            softmaxed = softmax_keys(q_blocks, k[rows], bias_ref)
            weights = softmaxed.astype(BF16)
            contexts.append(gather_heads(tn(weights, v[rows])).astype(BF16))
            grad_weights = nt(v[rows], g_blocks)
            inner = jnp.sum(grad_weights * softmaxed, axis=0, keepdims=True)
            grad_scores = (softmaxed * (grad_weights - inner)).astype(BF16)
            gqs.append((gather_heads(tn(grad_scores, k[rows])) * 0.125).astype(BF16))
            gks.append(nn(grad_scores, q_blocks).astype(BF16))
            gvs.append(nn(weights, g_blocks).astype(BF16))
        context = jnp.concatenate(contexts, axis=0)
        low_out += nt(context, od_ref[:, own])
        for i, parts in enumerate((gqs, gks, gvs)):
            gp = jnp.concatenate(parts, axis=0)
            gp_ref[:, columns(i, g)] = gp
            grads_ref[g, 8 * i : 8 * i + 8] = nn(lowt, gp)
            cl += nt(gp, pu_ref[:, columns(i, g)])
        grads_ref[g, 24:32] = nn(clot, context)
    clq_ref[...] = cl.astype(BF16)
    down = nn(cl.T.astype(BF16), normed)
    up = nn(low_out.T.astype(BF16), cot)
    for g in range(NG):
        grads_ref[g, 32:40] = down[:, g * GW : (g + 1) * GW]
        grads_ref[g, 40:48] = up[:, g * GW : (g + 1) * GW]


def input_grad_kernel(
    x_ref, gain_ref, gp_ref, wqkv_ref, clq_ref, pd_ref, o0, o1, o2, o3, o4, rows_ref
):
    standard, inv_std = layer_norm(x_ref[...])
    grad_normed = nt(gp_ref[...], wqkv_ref[...]) + nn(clq_ref[...], pd_ref[...])
    grad_hat = grad_normed * gain_ref[...]
    along = jnp.mean(grad_hat * standard, axis=-1, keepdims=True)
    mean = jnp.mean(grad_hat, axis=-1, keepdims=True)
    rows_ref[...] = inv_std * (grad_hat - mean - standard * along)
    take_apart(rows_ref, (o0, o1, o2, o3, o4))


def clip_kernel(first_ref, mine_ref, other_ref, qd_ref, qu_ref, od_ref, ou_ref):
    mine, other = mine_ref[...].astype(F32), other_ref[...].astype(F32)
    total = jnp.sum(jnp.sum(mine * mine, axis=(0, 1)) + jnp.sum(other * other, axis=(0, 1)))
    limit = jnp.sqrt(jnp.full((8, GW), 6.0 * D * RANK, F32))
    factor = jnp.minimum(1.0, limit / (jnp.sqrt(jnp.full((8, GW), total)) + 1e-06))
    is_first = first_ref[0] == 0
    for g in range(NG):
        own = mine[g % 2]
        far = other[g % 2]
        part = jnp.where(is_first, own, far) if g < 2 else jnp.where(is_first, far, own)
        cols = slice(g * GW, (g + 1) * GW)
        for i in range(3):
            qu_ref[:, columns(i, g)] = part[8 * i : 8 * i + 8] * factor
        od_ref[:, cols] = part[24:32] * factor
        qd_ref[:, cols] = part[32:40] * factor
        ou_ref[:, cols] = part[40:48] * factor


SMEM_SPEC = pl.BlockSpec(memory_space=pltpu.SMEM)
VMEM_SPEC = pl.BlockSpec(memory_space=pltpu.VMEM)
PIECES = (72, 108, 36, 36, 36)


def call(kernel, name, scalars, arrays, outs, scratch):
    return pl.pallas_call(
        kernel,
        in_specs=[SMEM_SPEC] * len(scalars) + [VMEM_SPEC] * len(arrays),
        out_specs=[VMEM_SPEC] * len(outs),
        out_shape=[jax.ShapeDtypeStruct(shape, dtype) for shape, dtype in outs],
        scratch_shapes=scratch,
        compiler_params=pltpu.CompilerParams(vmem_limit_bytes=VMEM),
        name=name,
    )(*scalars, *arrays)


PIECE_OUTS = [((rows, D), BF16) for rows in PIECES]
ROWS_SCRATCH = pltpu.VMEM((TOK, D), F32)
BIAS_SCRATCH = pltpu.VMEM((WIN, GQ), F32)


def run_forward(polar, x, weights):
    return call(
        forward_kernel, "forward", [polar], [*x, *weights], PIECE_OUTS, [ROWS_SCRATCH, BIAS_SCRATCH]
    )


def run_grads(polar, x, cot, weights):
    outs = [((TOK, D), F32), ((TOK, 3 * D), BF16), ((TOK, RANK), BF16), ((NG, 48, GW), F32)]
    return call(
        grads_kernel, "grads", [polar], [*x, *cot, *weights], outs, [ROWS_SCRATCH, BIAS_SCRATCH]
    )


def run_input_grad(x, gp, clq, weights):
    gain, wqkv, _, pd, _, _, _ = weights
    return call(
        input_grad_kernel, "input_grad", [], [x, gain, gp, wqkv, clq, pd], PIECE_OUTS, [ROWS_SCRATCH]
    )


def run_clip(first, mine, other):
    outs = [((RANK, n), F32) for n in (D, 3 * D, D, D)]
    return call(clip_kernel, "clip", [first], [mine, other], outs, [])


def shifted(block, lon, lat):
    n_lon, n_lat = lax.axis_size("lon"), lax.axis_size("lat")
    route = [
        (((i + lon) % n_lon) * n_lat + (j + lat) % n_lat, i * n_lat + j)
        for i in range(n_lon)
        for j in range(n_lat)
    ]
    return lax.ppermute(block, ("lon", "lat"), route)


def tokens(block):
    return block.reshape(-1, D)


def gather_windows(field):
    field = jnp.transpose(field, (1, 2, 0, 3))
    below = shifted(jnp.concatenate([tokens(field[:6, 3:9]), tokens(field[:6, 9:])]), 0, 1)
    corner = shifted(tokens(field[:6, :3]), 1, 1)
    side = shifted(tokens(field[6:, :3]), 1, 0)
    return tokens(field[6:, 3:9]), below, corner, tokens(field[6:, 9:]), side


def scatter_windows(pieces):
    own0, below, corner, own1, side = pieces
    below = shifted(below, 0, -1)
    side = shifted(side, -1, 0)
    corner = shifted(corner, -1, -1)
    grid6 = lambda a: a.reshape(6, 6, 2, D)
    grid3 = lambda a: a.reshape(6, 3, 2, D)
    upper = jnp.concatenate([grid3(corner), grid6(below[:72]), grid3(below[72:])], axis=1)
    lower = jnp.concatenate([grid3(side), grid6(own0), grid3(own1)], axis=1)
    return jnp.concatenate([upper, lower], axis=0)


def add_back(field, rows):
    back = jnp.transpose(scatter_windows(rows), (2, 0, 1, 3))
    return (field.astype(F32) + back.astype(F32)).astype(BF16)


def partner(block, lon_bit, lat_bit):
    n_lon, n_lat = lax.axis_size("lon"), lax.axis_size("lat")
    route = [
        ((i ^ lon_bit) * n_lat + (j ^ lat_bit), i * n_lat + j) for i in range(n_lon) for j in range(n_lat)
    ]
    return lax.ppermute(block, ("lon", "lat"), route)


def exchange(block, pairs):
    sent = block.astype(BF16)
    got = [partner(sent, a, b) for a, b in pairs]
    total = sent.astype(F32)
    for other in got:
        total = total + other.astype(F32)
    return total


def reduce_grads(grads):
    core = lax.rem(lax.axis_index("lon"), 2)
    halves = grads[:2], grads[2:]
    kept = jnp.where(core == 0, halves[0], halves[1])
    sent = jnp.where(core == 0, halves[1], halves[0]).astype(BF16)
    total = kept + partner(sent, 1, 0).astype(F32)
    n_lon, n_lat = lax.axis_size("lon"), lax.axis_size("lat")
    bits = [(b, 0) for b in (2, 4, 8) if b < n_lon] + [(0, b) for b in (1, 2, 4, 8) if b < n_lat]
    for pair in bits:
        total = exchange(total, [pair])
    total = total.astype(BF16)
    return total, partner(total, 1, 0), core


def per_device(input_a, input_b, cot_b, gain, wqkv, wo, pd, pu, od, ou):
    lat, n_lat = lax.axis_index("lat"), lax.axis_size("lat")
    polar = (lat == n_lat - 1).astype(jnp.int32).reshape(1)
    weights = (gain.reshape(1, D), wqkv, wo, pd.T, pu, od.T, ou)

    x_b = gather_windows(input_b)
    cot = gather_windows(cot_b)
    rows_b, gp, clq, grads = run_grads(polar, x_b, cot, weights)
    mine, other, core = reduce_grads(grads)

    x_a = gather_windows(input_a)
    output_a = add_back(input_a, run_forward(polar, x_a, weights))
    input_grad_b = add_back(cot_b, run_input_grad(rows_b, gp, clq, weights))

    qd, qu, od_grad, ou_grad = run_clip(core.reshape(1), mine, other)
    return output_a, input_grad_b, qd.T, qu, od_grad.T, ou_grad


def solution(mesh):
    field = P(None, "lat", "lon", None)
    return jax.shard_map(
        per_device,
        mesh=mesh,
        in_specs=(field,) * 3 + (P(),) * 7,
        out_specs=(field, field, P(), P(), P(), P()),
        check_vma=False,
    )
```

```python
import functools

import jax
import jax.numpy as jnp
from jax import lax
from jax.experimental import pallas as pl
from jax.experimental.pallas import tpu as pltpu
from jax.sharding import PartitionSpec as P

D = 1024
HD = 64
RANK = 8
TOK = 288
WIN = 144
HALF = 72
GH = 4
GW = GH * HD
NG = D // GW
GQ = GH * WIN
EPS = 1e-05
MASKED = -1e30
VMEM = 10 * 1024 * 1024
F32 = jnp.float32
BF16 = jnp.bfloat16


def nn(a, b):
    return jnp.dot(a, b, preferred_element_type=F32)


def nt(a, b):
    return lax.dot_general(a, b, (((1,), (1,)), ((), ())), preferred_element_type=F32)


def tn(a, b):
    return lax.dot_general(a, b, (((0,), (0,)), ((), ())), preferred_element_type=F32)


def layer_norm(tokens):
    average = jnp.mean(tokens, axis=-1, keepdims=True)
    centered = tokens - average
    variance = jnp.mean(centered * centered, axis=-1, keepdims=True)
    inv_std = lax.rsqrt(variance + EPS)
    return centered * inv_std, inv_std


def assemble(pieces, out_ref):
    at = 0
    for piece in pieces:
        rows = piece.shape[-2]
        out_ref[at : at + rows] = piece[...].astype(F32)
        at += rows


def take_apart(rows_ref, pieces):
    at = 0
    for piece in pieces:
        rows = piece.shape[-2]
        piece[...] = rows_ref[at : at + rows].astype(BF16)
        at += rows


def head_lanes(h):
    lane = lax.broadcasted_iota(jnp.int32, (1, GW), 1)
    return (lane >= h * HD) & (lane < (h + 1) * HD)


def spread_heads(a):
    zero = jnp.zeros_like(a)
    return jnp.concatenate([jnp.where(head_lanes(h), a, zero) for h in range(GH)], axis=0)


def gather_heads(a):
    out = a[:WIN]
    for h in range(1, GH):
        out = jnp.where(head_lanes(h), a[h * WIN : (h + 1) * WIN], out)
    return out


def pole_bias(polar):
    key = lax.broadcasted_iota(jnp.int32, (WIN, GQ), 0)
    query = lax.broadcasted_iota(jnp.int32, (WIN, GQ), 1)
    for h in range(1, GH):
        query = jnp.where(query >= WIN, query - WIN, query)
    apart = jnp.not_equal(key < HALF, query < HALF)
    return jnp.where(apart & (polar != 0), MASKED, 0.0)


def softmax_keys(q_blocks, k, bias_ref):
    scores = nt(k, q_blocks) + bias_ref[...]
    top = jnp.max(scores, axis=0, keepdims=True)
    p = jnp.exp(scores - top)
    return p * (1.0 / jnp.sum(p, axis=0, keepdims=True))


def project(normed, low, w_ref, up_ref, cols):
    return (nn(normed, w_ref[:, cols]) + nn(low, up_ref[:, cols])).astype(BF16)


def columns(i, g):
    return slice(i * D + g * GW, i * D + (g + 1) * GW)


def pack_kernel(*refs):
    sources, outs, fields, sems = refs[:3], refs[3:8], refs[8:11], refs[11]
    copies = [pltpu.make_async_copy(a, b, sems.at[i]) for i, (a, b) in enumerate(zip(sources, fields))]
    for copy in copies:
        copy.start()
    for copy in copies:
        copy.wait()
    *belows, corner, side = outs
    for i, field in enumerate(fields):
        below = belows[i].at[0]
        below[:72] = field[:6, 3:9].reshape(72, D)
        below[72:] = field[:6, 9:].reshape(36, D)
        corner[i] = field[:6, :3].reshape(36, D)
        side[i] = field[6:, :3].reshape(36, D)


def stage_kernel(*refs):
    sources, outs, sems = refs[:2], refs[2:4], refs[4]
    copies = [pltpu.make_async_copy(a, b, sems.at[i]) for i, (a, b) in enumerate(zip(sources, outs))]
    for copy in copies:
        copy.start()
    for copy in copies:
        copy.wait()


def pieces_of(field, below, corner, side):
    own0 = field[6:, 3:9].reshape(72, D)
    own1 = field[6:, 9:].reshape(36, D)
    return own0, below[...], corner[...], own1, side[...]


def attend_group(normed, low, wqkv_ref, pu_ref, bias_ref, g):
    q = project(normed, low, wqkv_ref, pu_ref, columns(0, g)) * 0.125
    k = project(normed, low, wqkv_ref, pu_ref, columns(1, g))
    v = project(normed, low, wqkv_ref, pu_ref, columns(2, g))
    contexts = []
    for w in range(2):
        rows = slice(w * WIN, (w + 1) * WIN)
        weights = softmax_keys(spread_heads(q[rows]), k[rows], bias_ref).astype(BF16)
        contexts.append(gather_heads(tn(weights, v[rows])).astype(BF16))
    return jnp.concatenate(contexts, axis=0)


def forward_first_kernel(
    polar_ref, field, below, corner, side, gain_ref, wqkv_ref, pd_ref, pu_ref,
    normed_ref, low_ref, context_ref, x_ref, bias_ref,
):
    assemble(pieces_of(field, below.at[0], corner.at[2], side.at[2]), x_ref)
    standard, _ = layer_norm(x_ref[...])
    normed = (standard * gain_ref[...]).astype(BF16)
    normed_ref[...] = normed
    low = nt(normed, pd_ref[...]).astype(BF16)
    low_ref[...] = low
    bias_ref[...] = pole_bias(polar_ref[0])
    for g in range(NG // 2):
        context_ref[:, columns(0, g)] = attend_group(normed, low, wqkv_ref, pu_ref, bias_ref, g)


def forward_second_kernel(
    polar_ref, normed_ref, low_ref, context_ref, wqkv_ref, wo_ref, pu_ref, od_ref, ou_ref, below_b,
    corner_b, side_b, own0, below, corner, own1, side, rows_ref, bias_ref,
):
    bias_ref[...] = pole_bias(polar_ref[0])
    normed, low = normed_ref[...], low_ref[...]
    groups = [
        attend_group(normed, low, wqkv_ref, pu_ref, bias_ref, g) for g in range(NG // 2, NG)
    ]
    context = jnp.concatenate([context_ref[...], *groups], axis=1)
    low_out = nt(context, od_ref[...]).astype(BF16)
    rows_ref[...] = nn(context, wo_ref[...]) + nn(low_out, ou_ref[...])
    take_apart(rows_ref, [a.at[0] for a in (own0, below, corner, own1, side)])
    below[1] = below_b[...]
    corner[1] = corner_b[...]
    side[1] = side_b[...]


def encode_kernel(
    polar_ref, field, below, corner, side, gain_ref, wqkv_ref, pd_ref, pu_ref, od_ref,
    x_ref, normed_ref, lowt_ref, qkv_ref, soft_ref, context_ref, lowt_out_ref, bias_ref,
):
    assemble(pieces_of(field, below.at[0], corner.at[0], side.at[0]), x_ref)
    standard, _ = layer_norm(x_ref[...])
    normed = (standard * gain_ref[...]).astype(BF16)
    normed_ref[...] = normed
    low = nt(normed, pd_ref[...])
    lowt_ref[...] = low.T.astype(BF16)
    low = low.astype(BF16)
    bias_ref[...] = pole_bias(polar_ref[0])
    low_out = jnp.zeros((TOK, RANK), F32)
    for g in range(NG):
        q = project(normed, low, wqkv_ref, pu_ref, columns(0, g)) * 0.125
        k = project(normed, low, wqkv_ref, pu_ref, columns(1, g))
        v = project(normed, low, wqkv_ref, pu_ref, columns(2, g))
        for i, a in enumerate((q, k, v)):
            qkv_ref[:, columns(i, g)] = a
        contexts = []
        for w in range(2):
            rows = slice(w * WIN, (w + 1) * WIN)
            softmaxed = softmax_keys(spread_heads(q[rows]), k[rows], bias_ref)
            soft_ref[2 * g + w] = softmaxed
            contexts.append(gather_heads(tn(softmaxed.astype(BF16), v[rows])).astype(BF16))
        context = jnp.concatenate(contexts, axis=0)
        context_ref[:, columns(0, g)] = context
        low_out += nt(context, od_ref[:, columns(0, g)])
    lowt_out_ref[...] = low_out.T.astype(BF16)


def grads_kernel(
    field, below, corner, side, normed_ref, lowt_ref, qkv_ref, soft_ref, context_ref, lowt_out_ref,
    wo_ref, pu_ref, od_ref, ou_ref, gp_ref, clq_ref, grads_ref, rows_ref,
):
    assemble(pieces_of(field, below.at[0], corner.at[1], side.at[1]), rows_ref)
    cot = rows_ref[...].astype(BF16)
    clo = nt(cot, ou_ref[...])
    clot = clo.T.astype(BF16)
    clo = clo.astype(BF16)
    lowt = lowt_ref[...]
    cl = jnp.zeros((TOK, RANK), F32)
    for g in range(NG):
        own = columns(0, g)
        q, k, v = (qkv_ref[:, columns(i, g)] for i in range(3))
        grad_context = (nt(cot, wo_ref[own, :]) + nn(clo, od_ref[:, own])).astype(BF16)
        gqs, gks, gvs = [], [], []
        for w in range(2):
            rows = slice(w * WIN, (w + 1) * WIN)
            q_blocks, g_blocks = spread_heads(q[rows]), spread_heads(grad_context[rows])
            softmaxed = soft_ref[2 * g + w]
            grad_weights = nt(v[rows], g_blocks)
            inner = jnp.sum(grad_weights * softmaxed, axis=0, keepdims=True)
            grad_scores = (softmaxed * (grad_weights - inner)).astype(BF16)
            gqs.append((gather_heads(tn(grad_scores, k[rows])) * 0.125).astype(BF16))
            gks.append(nn(grad_scores, q_blocks).astype(BF16))
            gvs.append(nn(softmaxed.astype(BF16), g_blocks).astype(BF16))
        for i, parts in enumerate((gqs, gks, gvs)):
            gp = jnp.concatenate(parts, axis=0)
            gp_ref[:, columns(i, g)] = gp
            grads_ref[g, 8 * i : 8 * i + 8] = nn(lowt, gp)
            cl += nt(gp, pu_ref[:, columns(i, g)])
        grads_ref[g, 24:32] = nn(clot, context_ref[:, own])
    clq_ref[...] = cl.astype(BF16)
    down = nn(cl.T.astype(BF16), normed_ref[...])
    up = nn(lowt_out_ref[...], cot)
    for g in range(NG):
        grads_ref[g, 32:40] = down[:, g * GW : (g + 1) * GW]
        grads_ref[g, 40:48] = up[:, g * GW : (g + 1) * GW]


def input_grad_kernel(
    x_ref, gain_ref, gp_ref, wqkv_ref, clq_ref, pd_ref, o0, o1, o2, o3, o4, rows_ref
):
    standard, inv_std = layer_norm(x_ref[...])
    grad_normed = nt(gp_ref[...], wqkv_ref[...]) + nn(clq_ref[...], pd_ref[...])
    grad_hat = grad_normed * gain_ref[...]
    along = jnp.mean(grad_hat * standard, axis=-1, keepdims=True)
    mean = jnp.mean(grad_hat, axis=-1, keepdims=True)
    rows_ref[...] = inv_std * (grad_hat - mean - standard * along)
    take_apart(rows_ref, (o0, o1, o2, o3, o4))


def clip_kernel(first_ref, mine_ref, other_ref, qd_ref, qu_ref, od_ref, ou_ref):
    mine, other = mine_ref[...].astype(F32), other_ref[...].astype(F32)
    total = jnp.sum(jnp.sum(mine * mine, axis=(0, 1)) + jnp.sum(other * other, axis=(0, 1)))
    limit = jnp.sqrt(jnp.full((8, GW), 6.0 * D * RANK, F32))
    factor = jnp.minimum(1.0, limit / (jnp.sqrt(jnp.full((8, GW), total)) + 1e-06))
    is_first = first_ref[0] == 0
    for g in range(NG):
        own = mine[g % 2]
        far = other[g % 2]
        part = jnp.where(is_first, own, far) if g < 2 else jnp.where(is_first, far, own)
        cols = slice(g * GW, (g + 1) * GW)
        for i in range(3):
            qu_ref[:, columns(i, g)] = part[8 * i : 8 * i + 8] * factor
        od_ref[:, cols] = part[24:32] * factor
        qd_ref[:, cols] = part[32:40] * factor
        ou_ref[:, cols] = part[40:48] * factor


SMEM_SPEC = pl.BlockSpec(memory_space=pltpu.SMEM)
VMEM_SPEC = pl.BlockSpec(memory_space=pltpu.VMEM)
PIECES = (72, 108, 36, 36, 36)


def cost(us):
    return pl.CostEstimate(flops=us * 1000000000, bytes_accessed=4000000, transcendentals=0)


def call(kernel, name, us, scalars, arrays, outs, scratch):
    return pl.pallas_call(
        kernel,
        in_specs=[SMEM_SPEC] * len(scalars) + [VMEM_SPEC] * len(arrays),
        out_specs=[VMEM_SPEC] * len(outs),
        out_shape=[jax.ShapeDtypeStruct(shape, dtype) for shape, dtype in outs],
        scratch_shapes=scratch,
        compiler_params=pltpu.CompilerParams(vmem_limit_bytes=VMEM),
        cost_estimate=cost(us),
        name=name,
    )(*scalars, *arrays)


PIECE_OUTS = [((rows, D), BF16) for rows in PIECES]
ROWS_SCRATCH = pltpu.VMEM((TOK, D), F32)
BIAS_SCRATCH = pltpu.VMEM((WIN, GQ), F32)


def run_pack(x_b, cot, x_a):
    fields = [pltpu.with_memory_space_constraint(a, pltpu.HBM) for a in (x_b, cot, x_a)]
    return pl.pallas_call(
        pack_kernel,
        in_specs=[pl.BlockSpec(memory_space=pltpu.HBM)] * 3,
        out_specs=[VMEM_SPEC] * 5,
        out_shape=[
            jax.ShapeDtypeStruct(shape, BF16)
            for shape in ((1, 108, D), (1, 108, D), (1, 108, D), (3, 36, D), (3, 36, D))
        ],
        scratch_shapes=[
            *[pltpu.VMEM((12, 12, 2, D), BF16) for _ in range(3)],
            pltpu.SemaphoreType.DMA((3,)),
        ],
        compiler_params=pltpu.CompilerParams(vmem_limit_bytes=VMEM),
        cost_estimate=cost(20),
        name="pack",
    )(*fields)


def run_stage(wqkv, wo):
    return pl.pallas_call(
        stage_kernel,
        in_specs=[pl.BlockSpec(memory_space=pltpu.HBM)] * 2,
        out_specs=[VMEM_SPEC] * 2,
        out_shape=[jax.ShapeDtypeStruct(a.shape, BF16) for a in (wqkv, wo)],
        scratch_shapes=[pltpu.SemaphoreType.DMA((2,))],
        compiler_params=pltpu.CompilerParams(vmem_limit_bytes=VMEM),
        cost_estimate=cost(3),
        name="stage",
    )(*[pltpu.with_memory_space_constraint(a, pltpu.HBM) for a in (wqkv, wo)])


def run_forward_first(polar, field, halo, weights):
    gain, wqkv, _, pd, pu, _, _ = weights
    outs = [((TOK, D), BF16), ((TOK, RANK), BF16), ((TOK, D // 2), BF16)]
    arrays = [field, *halo, gain, wqkv, pd, pu]
    scratch = [ROWS_SCRATCH, BIAS_SCRATCH]
    return call(forward_first_kernel, "forward_first", 4, [polar], arrays, outs, scratch)


def run_forward_second(polar, saved, pieces_b, weights):
    _, wqkv, wo, _, pu, od, ou = weights
    outs = [((n, rows, D), BF16) for n, rows in ((1, 72), (2, 108), (2, 36), (1, 36), (2, 36))]
    arrays = [*saved, wqkv, wo, pu, od, ou, *pieces_b]
    scratch = [ROWS_SCRATCH, BIAS_SCRATCH]
    return call(forward_second_kernel, "forward_second", 4, [polar], arrays, outs, scratch)


def run_encode(polar, field, halo, weights):
    gain, wqkv, _, pd, pu, od, _ = weights
    outs = [
        ((TOK, D), F32),
        ((TOK, D), BF16),
        ((RANK, TOK), BF16),
        ((TOK, 3 * D), BF16),
        ((2 * NG, WIN, GQ), F32),
        ((TOK, D), BF16),
        ((RANK, TOK), BF16),
    ]
    arrays = [field, *halo, gain, wqkv, pd, pu, od]
    return call(encode_kernel, "encode", 7, [polar], arrays, outs, [BIAS_SCRATCH])


def run_grads(field, halo, saved, weights):
    _, _, wo, _, pu, od, ou = weights
    outs = [((TOK, 3 * D), BF16), ((TOK, RANK), BF16), ((NG, 48, GW), F32)]
    arrays = [field, *halo, *saved, wo, pu, od, ou]
    return call(grads_kernel, "grads", 7, [], arrays, outs, [ROWS_SCRATCH])


def run_input_grad(x, gp, clq, weights):
    gain, wqkv, _, pd, _, _, _ = weights
    return call(
        input_grad_kernel, "input_grad", 3, [], [x, gain, gp, wqkv, clq, pd], PIECE_OUTS, [ROWS_SCRATCH]
    )


def run_clip(first, mine, other):
    outs = [((RANK, n), F32) for n in (D, 3 * D, D, D)]
    return call(clip_kernel, "clip", 1, [first], [mine, other], outs, [])


def shifted(block, lon, lat):
    n_lon, n_lat = lax.axis_size("lon"), lax.axis_size("lat")
    route = [
        (((i + lon) % n_lon) * n_lat + (j + lat) % n_lat, i * n_lat + j)
        for i in range(n_lon)
        for j in range(n_lat)
    ]
    return lax.ppermute(block, ("lon", "lat"), route)


def add_back(field, own0, below, corner, own1, side):
    grid6 = lambda a: a.reshape(6, 6, 2, D)
    grid3 = lambda a: a.reshape(6, 3, 2, D)
    upper = jnp.concatenate([grid3(corner), grid6(below[:72]), grid3(below[72:])], axis=1)
    lower = jnp.concatenate([grid3(side), grid6(own0), grid3(own1)], axis=1)
    back = jnp.transpose(jnp.concatenate([upper, lower], axis=0), (2, 0, 1, 3))
    return (field.astype(F32) + back.astype(F32)).astype(BF16)


def partner(block, lon_bit, lat_bit):
    n_lon, n_lat = lax.axis_size("lon"), lax.axis_size("lat")
    route = [
        ((i ^ lon_bit) * n_lat + (j ^ lat_bit), i * n_lat + j) for i in range(n_lon) for j in range(n_lat)
    ]
    return lax.ppermute(block, ("lon", "lat"), route)


def exchange(total, pair, work=None, args=()):
    sent = total.astype(BF16)
    if work is None:
        return sent.astype(F32) + partner(sent, *pair).astype(F32), None
    sent, args = lax.optimization_barrier((sent, args))
    got = partner(sent, *pair)
    got, done = lax.optimization_barrier((got, work(*args)))
    return sent.astype(F32) + got.astype(F32), done


def per_device(input_a, input_b, cot_b, gain, wqkv, wo, pd, pu, od, ou):
    n_lon, n_lat = lax.axis_size("lon"), lax.axis_size("lat")
    polar = (lax.axis_index("lat") == n_lat - 1).astype(jnp.int32).reshape(1)

    x_b, cot, x_a = (jnp.transpose(field, (1, 2, 0, 3)) for field in (input_b, cot_b, input_a))
    below_x, below_cot, below_a, corner, side = run_pack(x_b, cot, x_a)
    wqkv, wo, below_x = lax.optimization_barrier((wqkv, wo, below_x))
    staged = run_stage(wqkv, wo)
    below_x = shifted(below_x, 0, 1)
    corner = shifted(corner, 1, 1)
    side = shifted(side, 1, 0)
    wqkv, wo, below_x, corner, side, below_cot = lax.optimization_barrier(
        (*staged, below_x, corner, side, below_cot)
    )
    weights = (gain.reshape(1, D), wqkv, wo, pd.T, pu, od.T, ou)
    rows_b, *saved = run_encode(polar, x_b, (below_x, corner, side), weights)
    below_cot = shifted(below_cot, 0, 1)
    saved, below_cot, below_a = lax.optimization_barrier((saved, below_cot, below_a))
    gp, clq, grads = run_grads(cot, (below_cot, corner, side), saved, weights)
    below_a = shifted(below_a, 0, 1)

    core = lax.rem(lax.axis_index("lon"), 2)
    halves = grads[:2], grads[2:]
    kept = jnp.where(core == 0, halves[0], halves[1])
    sent = jnp.where(core == 0, halves[1], halves[0]).astype(BF16)
    total = kept + partner(sent, 1, 0).astype(F32)

    pairs = [(2, 0), (0, 1), (4, 0), (8, 0), (0, 2), (0, 4), (0, 8)]
    pairs = [(a, b) for a, b in pairs if a < n_lon and b < n_lat]
    total, (own0_b, below_b, corner_b, own1_b, side_b) = exchange(
        total, pairs[0], lambda *a: run_input_grad(*a, weights), (rows_b, gp, clq)
    )
    total, saved = exchange(
        total,
        pairs[1],
        lambda *halo: run_forward_first(polar, x_a, halo, weights),
        (below_a, corner, side),
    )
    total, (own0_a, below, corner, own1_a, side) = exchange(
        total,
        pairs[2],
        lambda *a: run_forward_second(polar, a[:3], a[3:], weights),
        (*saved, below_b, corner_b, side_b),
    )
    below = shifted(below, 0, -1)
    corner = shifted(corner, -1, -1)
    side = shifted(side, -1, 0)
    for pair in pairs[3:-1]:
        total = exchange(total, pair)[0]
    total, (output_a, input_grad_b) = exchange(
        total,
        pairs[-1],
        lambda below, corner, side: (
            add_back(input_a, own0_a, below[0], corner[0], own1_a, side[0]),
            add_back(cot_b, own0_b, below[1], corner[1], own1_b, side[1]),
        ),
        (below, corner, side),
    )
    total = total.astype(BF16)
    qd, qu, od_grad, ou_grad = run_clip(core.reshape(1), total, partner(total, 1, 0))
    return output_a, input_grad_b, qd.T, qu, od_grad.T, ou_grad


def solution(mesh):
    field = P(None, "lat", "lon", None)
    return jax.shard_map(
        per_device,
        mesh=mesh,
        in_specs=(field,) * 3 + (P(),) * 7,
        out_specs=(field, field, P(), P(), P(), P()),
        check_vma=False,
    )
```

```python
import functools

import jax
import jax.numpy as jnp
from jax import lax
from jax.experimental import pallas as pl
from jax.experimental.pallas import tpu as pltpu
from jax.sharding import PartitionSpec as P

D = 1024
HD = 64
RANK = 8
TOK = 288
WIN = 144
HALF = 72
GH = 4
GW = GH * HD
NG = D // GW
GQ = GH * WIN
EPS = 1e-05
MASKED = -1e30
VMEM = 10 * 1024 * 1024
F32 = jnp.float32
BF16 = jnp.bfloat16


def nn(a, b):
    return jnp.dot(a, b, preferred_element_type=F32)


def nt(a, b):
    return lax.dot_general(a, b, (((1,), (1,)), ((), ())), preferred_element_type=F32)


def tn(a, b):
    return lax.dot_general(a, b, (((0,), (0,)), ((), ())), preferred_element_type=F32)


def layer_norm(tokens):
    average = jnp.mean(tokens, axis=-1, keepdims=True)
    centered = tokens - average
    variance = jnp.mean(centered * centered, axis=-1, keepdims=True)
    inv_std = lax.rsqrt(variance + EPS)
    return centered * inv_std, inv_std


def assemble(pieces, out_ref):
    at = 0
    for piece in pieces:
        rows = piece.shape[-2]
        out_ref[at : at + rows] = piece[...].astype(F32)
        at += rows


def take_apart(rows_ref, pieces):
    at = 0
    for piece in pieces:
        rows = piece.shape[-2]
        piece[...] = rows_ref[at : at + rows].astype(BF16)
        at += rows


def head_lanes(h):
    lane = lax.broadcasted_iota(jnp.int32, (1, GW), 1)
    return (lane >= h * HD) & (lane < (h + 1) * HD)


def spread_heads(a):
    zero = jnp.zeros_like(a)
    return jnp.concatenate([jnp.where(head_lanes(h), a, zero) for h in range(GH)], axis=0)


def gather_heads(a):
    out = a[:WIN]
    for h in range(1, GH):
        out = jnp.where(head_lanes(h), a[h * WIN : (h + 1) * WIN], out)
    return out


def pole_bias(polar):
    key = lax.broadcasted_iota(jnp.int32, (WIN, GQ), 0)
    query = lax.broadcasted_iota(jnp.int32, (WIN, GQ), 1)
    for h in range(1, GH):
        query = jnp.where(query >= WIN, query - WIN, query)
    apart = jnp.not_equal(key < HALF, query < HALF)
    return jnp.where(apart & (polar != 0), MASKED, 0.0)


def softmax_keys(q_blocks, k, bias_ref):
    scores = nt(k, q_blocks) + bias_ref[...]
    top = jnp.max(scores, axis=0, keepdims=True)
    p = jnp.exp(scores - top)
    return p * (1.0 / jnp.sum(p, axis=0, keepdims=True))


def project(normed, low, w_ref, up_ref, cols):
    return (nn(normed, w_ref[:, cols]) + nn(low, up_ref[:, cols])).astype(BF16)


def columns(i, g):
    return slice(i * D + g * GW, i * D + (g + 1) * GW)


def copy_in(pairs, sems):
    copies = [pltpu.make_async_copy(a, b, sems.at[i]) for i, (a, b) in enumerate(pairs)]
    for copy in copies:
        copy.start()
    for copy in copies:
        copy.wait()


def cut_below(rows, out):
    out[:72] = rows[:, :6].reshape(72, D)
    out[72:] = rows[:, 6:].reshape(36, D)


def pack_kernel(x_b, cot, x_a, below, corner, side, upper, *rest):
    firsts, sems = rest[:3], rest[3]
    pairs = [(a.at[:, :3], b) for a, b in zip((x_b, cot, x_a), firsts)]
    copy_in([(x_b.at[:6, 3:], upper), *pairs], sems)
    cut_below(upper, below.at[0])
    for i, first in enumerate(firsts):
        corner[i] = first[:6].reshape(36, D)
        side[i] = first[6:].reshape(36, D)


def pack_rest_kernel(cot, x_a, below, first, second, sems):
    copy_in([(cot.at[:6, 3:], first), (x_a.at[:6, 3:], second)], sems)
    cut_below(first, below.at[0])
    cut_below(second, below.at[1])


def stage_kernel(*refs):
    copy_in(zip(refs[:2], refs[2:4]), refs[4])


def pieces_of(field, below, corner, side):
    own0 = field[6:, 3:9].reshape(72, D)
    own1 = field[6:, 9:].reshape(36, D)
    return own0, below[...], corner[...], own1, side[...]


def attend_group(normed, low, wqkv_ref, pu_ref, bias_ref, g):
    q = project(normed, low, wqkv_ref, pu_ref, columns(0, g)) * 0.125
    k = project(normed, low, wqkv_ref, pu_ref, columns(1, g))
    v = project(normed, low, wqkv_ref, pu_ref, columns(2, g))
    contexts = []
    for w in range(2):
        rows = slice(w * WIN, (w + 1) * WIN)
        weights = softmax_keys(spread_heads(q[rows]), k[rows], bias_ref).astype(BF16)
        contexts.append(gather_heads(tn(weights, v[rows])).astype(BF16))
    return jnp.concatenate(contexts, axis=0)


def forward_first_kernel(
    polar_ref, field, below, corner, side, gain_ref, wqkv_ref, pd_ref, pu_ref,
    normed_ref, low_ref, context_ref, x_ref, bias_ref,
):
    assemble(pieces_of(field, below.at[1], corner.at[2], side.at[2]), x_ref)
    standard, _ = layer_norm(x_ref[...])
    normed = (standard * gain_ref[...]).astype(BF16)
    normed_ref[...] = normed
    low = nt(normed, pd_ref[...]).astype(BF16)
    low_ref[...] = low
    bias_ref[...] = pole_bias(polar_ref[0])
    for g in range(NG // 2):
        context_ref[:, columns(0, g)] = attend_group(normed, low, wqkv_ref, pu_ref, bias_ref, g)


def forward_second_kernel(
    polar_ref, normed_ref, low_ref, context_ref, wqkv_ref, wo_ref, pu_ref, od_ref, ou_ref, below_b,
    corner_b, side_b, own0, below, corner, own1, side, rows_ref, bias_ref,
):
    bias_ref[...] = pole_bias(polar_ref[0])
    normed, low = normed_ref[...], low_ref[...]
    groups = [
        attend_group(normed, low, wqkv_ref, pu_ref, bias_ref, g) for g in range(NG // 2, NG)
    ]
    context = jnp.concatenate([context_ref[...], *groups], axis=1)
    low_out = nt(context, od_ref[...]).astype(BF16)
    rows_ref[...] = nn(context, wo_ref[...]) + nn(low_out, ou_ref[...])
    take_apart(rows_ref, [a.at[0] for a in (own0, below, corner, own1, side)])
    below[1] = below_b[...]
    corner[1] = corner_b[...]
    side[1] = side_b[...]


def encode_kernel(
    polar_ref, field, below, corner, side, gain_ref, wqkv_ref, pd_ref, pu_ref, od_ref,
    x_ref, normed_ref, lowt_ref, qkv_ref, soft_ref, context_ref, lowt_out_ref, bias_ref,
):
    assemble(pieces_of(field, below.at[0], corner.at[0], side.at[0]), x_ref)
    standard, _ = layer_norm(x_ref[...])
    normed = (standard * gain_ref[...]).astype(BF16)
    normed_ref[...] = normed
    low = nt(normed, pd_ref[...])
    lowt_ref[...] = low.T.astype(BF16)
    low = low.astype(BF16)
    bias_ref[...] = pole_bias(polar_ref[0])
    low_out = jnp.zeros((TOK, RANK), F32)
    for g in range(NG):
        q = project(normed, low, wqkv_ref, pu_ref, columns(0, g)) * 0.125
        k = project(normed, low, wqkv_ref, pu_ref, columns(1, g))
        v = project(normed, low, wqkv_ref, pu_ref, columns(2, g))
        for i, a in enumerate((q, k, v)):
            qkv_ref[:, columns(i, g)] = a
        contexts = []
        for w in range(2):
            rows = slice(w * WIN, (w + 1) * WIN)
            softmaxed = softmax_keys(spread_heads(q[rows]), k[rows], bias_ref)
            soft_ref[2 * g + w] = softmaxed
            contexts.append(gather_heads(tn(softmaxed.astype(BF16), v[rows])).astype(BF16))
        context = jnp.concatenate(contexts, axis=0)
        context_ref[:, columns(0, g)] = context
        low_out += nt(context, od_ref[:, columns(0, g)])
    lowt_out_ref[...] = low_out.T.astype(BF16)


def grads_kernel(
    field, below, corner, side, normed_ref, lowt_ref, qkv_ref, soft_ref, context_ref, lowt_out_ref,
    wo_ref, pu_ref, od_ref, ou_ref, gp_ref, clq_ref, grads_ref, rows_ref,
):
    assemble(pieces_of(field, below.at[0], corner.at[1], side.at[1]), rows_ref)
    cot = rows_ref[...].astype(BF16)
    clo = nt(cot, ou_ref[...])
    clot = clo.T.astype(BF16)
    clo = clo.astype(BF16)
    lowt = lowt_ref[...]
    cl = jnp.zeros((TOK, RANK), F32)
    for g in range(NG):
        own = columns(0, g)
        q, k, v = (qkv_ref[:, columns(i, g)] for i in range(3))
        grad_context = (nt(cot, wo_ref[own, :]) + nn(clo, od_ref[:, own])).astype(BF16)
        gqs, gks, gvs = [], [], []
        for w in range(2):
            rows = slice(w * WIN, (w + 1) * WIN)
            q_blocks, g_blocks = spread_heads(q[rows]), spread_heads(grad_context[rows])
            softmaxed = soft_ref[2 * g + w]
            grad_weights = nt(v[rows], g_blocks)
            inner = jnp.sum(grad_weights * softmaxed, axis=0, keepdims=True)
            grad_scores = (softmaxed * (grad_weights - inner)).astype(BF16)
            gqs.append((gather_heads(tn(grad_scores, k[rows])) * 0.125).astype(BF16))
            gks.append(nn(grad_scores, q_blocks).astype(BF16))
            gvs.append(nn(softmaxed.astype(BF16), g_blocks).astype(BF16))
        for i, parts in enumerate((gqs, gks, gvs)):
            gp = jnp.concatenate(parts, axis=0)
            gp_ref[:, columns(i, g)] = gp
            grads_ref[g, 8 * i : 8 * i + 8] = nn(lowt, gp)
            cl += nt(gp, pu_ref[:, columns(i, g)])
        grads_ref[g, 24:32] = nn(clot, context_ref[:, own])
    clq_ref[...] = cl.astype(BF16)
    down = nn(cl.T.astype(BF16), normed_ref[...])
    up = nn(lowt_out_ref[...], cot)
    for g in range(NG):
        grads_ref[g, 32:40] = down[:, g * GW : (g + 1) * GW]
        grads_ref[g, 40:48] = up[:, g * GW : (g + 1) * GW]


def input_grad_kernel(
    x_ref, gain_ref, gp_ref, wqkv_ref, clq_ref, pd_ref, o0, o1, o2, o3, o4, rows_ref
):
    standard, inv_std = layer_norm(x_ref[...])
    grad_normed = nt(gp_ref[...], wqkv_ref[...]) + nn(clq_ref[...], pd_ref[...])
    grad_hat = grad_normed * gain_ref[...]
    along = jnp.mean(grad_hat * standard, axis=-1, keepdims=True)
    mean = jnp.mean(grad_hat, axis=-1, keepdims=True)
    rows_ref[...] = inv_std * (grad_hat - mean - standard * along)
    take_apart(rows_ref, (o0, o1, o2, o3, o4))


def add_kernel(field_a, field_b, own0_a, own1_a, own0_b, own1_b, below, corner, side, out_a, out_b):
    parts = ((field_a, own0_a.at[0], own1_a.at[0], out_a), (field_b, own0_b, own1_b, out_b))
    for i, (field, own0, own1, out) in enumerate(parts):
        places = (
            (slice(0, 6), slice(0, 3), corner[i]),
            (slice(0, 6), slice(3, 9), below[i, :72]),
            (slice(0, 6), slice(9, 12), below[i, 72:]),
            (slice(6, 12), slice(0, 3), side[i]),
            (slice(6, 12), slice(3, 9), own0[...]),
            (slice(6, 12), slice(9, 12), own1[...]),
        )
        for rows, cols, piece in places:
            here = field[rows, cols]
            out[rows, cols] = (here.astype(F32) + piece.reshape(here.shape).astype(F32)).astype(BF16)


def clip_kernel(first_ref, mine_ref, other_ref, qd_ref, qu_ref, od_ref, ou_ref):
    mine, other = mine_ref[...].astype(F32), other_ref[...].astype(F32)
    total = jnp.sum(jnp.sum(mine * mine, axis=(0, 1)) + jnp.sum(other * other, axis=(0, 1)))
    limit = jnp.sqrt(jnp.full((8, GW), 6.0 * D * RANK, F32))
    factor = jnp.minimum(1.0, limit / (jnp.sqrt(jnp.full((8, GW), total)) + 1e-06))
    is_first = first_ref[0] == 0
    for g in range(NG):
        own = mine[g % 2]
        far = other[g % 2]
        part = jnp.where(is_first, own, far) if g < 2 else jnp.where(is_first, far, own)
        cols = slice(g * GW, (g + 1) * GW)
        for i in range(3):
            qu_ref[:, columns(i, g)] = part[8 * i : 8 * i + 8] * factor
        od_ref[:, cols] = part[24:32] * factor
        qd_ref[:, cols] = part[32:40] * factor
        ou_ref[:, cols] = part[40:48] * factor


SMEM_SPEC = pl.BlockSpec(memory_space=pltpu.SMEM)
VMEM_SPEC = pl.BlockSpec(memory_space=pltpu.VMEM)
PIECES = (72, 108, 36, 36, 36)


def cost(us):
    return pl.CostEstimate(flops=us * 1000000000, bytes_accessed=4000000, transcendentals=0)


def call(kernel, name, us, scalars, arrays, outs, scratch):
    return pl.pallas_call(
        kernel,
        in_specs=[SMEM_SPEC] * len(scalars) + [VMEM_SPEC] * len(arrays),
        out_specs=[VMEM_SPEC] * len(outs),
        out_shape=[jax.ShapeDtypeStruct(shape, dtype) for shape, dtype in outs],
        scratch_shapes=scratch,
        compiler_params=pltpu.CompilerParams(vmem_limit_bytes=VMEM),
        cost_estimate=cost(us),
        name=name,
    )(*scalars, *arrays)


PIECE_OUTS = [((rows, D), BF16) for rows in PIECES]
ROWS_SCRATCH = pltpu.VMEM((TOK, D), F32)
BIAS_SCRATCH = pltpu.VMEM((WIN, GQ), F32)


def call_far(kernel, name, us, arrays, outs, buffers, copies):
    return pl.pallas_call(
        kernel,
        in_specs=[pl.BlockSpec(memory_space=pltpu.HBM)] * len(arrays),
        out_specs=[VMEM_SPEC] * len(outs),
        out_shape=[jax.ShapeDtypeStruct(shape, BF16) for shape in outs],
        scratch_shapes=[
            *[pltpu.VMEM(shape, BF16) for shape in buffers],
            pltpu.SemaphoreType.DMA((copies,)),
        ],
        compiler_params=pltpu.CompilerParams(vmem_limit_bytes=VMEM),
        cost_estimate=cost(us),
        name=name,
    )(*[pltpu.with_memory_space_constraint(a, pltpu.HBM) for a in arrays])


def run_pack(x_b, cot, x_a):
    outs = [(1, 108, D), (3, 36, D), (3, 36, D)]
    buffers = [(6, 9, 2, D)] + [(12, 3, 2, D)] * 3
    return call_far(pack_kernel, "pack", 20, [x_b, cot, x_a], outs, buffers, 4)


def run_pack_rest(cot, x_a):
    return call_far(pack_rest_kernel, "pack_rest", 2, [cot, x_a], [(2, 108, D)], [(6, 9, 2, D)] * 2, 2)[0]


def run_stage(wqkv, wo):
    return call_far(stage_kernel, "stage", 3, [wqkv, wo], [wqkv.shape, wo.shape], [], 2)


def run_forward_first(polar, field, halo, weights):
    gain, wqkv, _, pd, pu, _, _ = weights
    outs = [((TOK, D), BF16), ((TOK, RANK), BF16), ((TOK, D // 2), BF16)]
    arrays = [field, *halo, gain, wqkv, pd, pu]
    scratch = [ROWS_SCRATCH, BIAS_SCRATCH]
    return call(forward_first_kernel, "forward_first", 4, [polar], arrays, outs, scratch)


def run_forward_second(polar, saved, pieces_b, weights):
    _, wqkv, wo, _, pu, od, ou = weights
    outs = [((n, rows, D), BF16) for n, rows in ((1, 72), (2, 108), (2, 36), (1, 36), (2, 36))]
    arrays = [*saved, wqkv, wo, pu, od, ou, *pieces_b]
    scratch = [ROWS_SCRATCH, BIAS_SCRATCH]
    return call(forward_second_kernel, "forward_second", 4, [polar], arrays, outs, scratch)


def run_encode(polar, field, halo, weights):
    gain, wqkv, _, pd, pu, od, _ = weights
    outs = [
        ((TOK, D), F32),
        ((TOK, D), BF16),
        ((RANK, TOK), BF16),
        ((TOK, 3 * D), BF16),
        ((2 * NG, WIN, GQ), F32),
        ((TOK, D), BF16),
        ((RANK, TOK), BF16),
    ]
    arrays = [field, *halo, gain, wqkv, pd, pu, od]
    return call(encode_kernel, "encode", 7, [polar], arrays, outs, [BIAS_SCRATCH])


def run_grads(field, halo, saved, weights):
    _, _, wo, _, pu, od, ou = weights
    outs = [((TOK, 3 * D), BF16), ((TOK, RANK), BF16), ((NG, 48, GW), F32)]
    arrays = [field, *halo, *saved, wo, pu, od, ou]
    return call(grads_kernel, "grads", 7, [], arrays, outs, [ROWS_SCRATCH])


def run_input_grad(x, gp, clq, weights):
    gain, wqkv, _, pd, _, _, _ = weights
    return call(
        input_grad_kernel, "input_grad", 3, [], [x, gain, gp, wqkv, clq, pd], PIECE_OUTS, [ROWS_SCRATCH]
    )


def run_add(*arrays):
    return call(add_kernel, "add", 3, [], arrays, [((12, 12, 2, D), BF16)] * 2, [])


def run_clip(first, mine, other):
    outs = [((RANK, n), F32) for n in (D, 3 * D, D, D)]
    return call(clip_kernel, "clip", 1, [first], [mine, other], outs, [])


def shifted(block, lon, lat):
    n_lon, n_lat = lax.axis_size("lon"), lax.axis_size("lat")
    route = [
        (((i + lon) % n_lon) * n_lat + (j + lat) % n_lat, i * n_lat + j)
        for i in range(n_lon)
        for j in range(n_lat)
    ]
    return lax.ppermute(block, ("lon", "lat"), route)


def partner(block, lon_bit, lat_bit):
    n_lon, n_lat = lax.axis_size("lon"), lax.axis_size("lat")
    route = [
        ((i ^ lon_bit) * n_lat + (j ^ lat_bit), i * n_lat + j) for i in range(n_lon) for j in range(n_lat)
    ]
    return lax.ppermute(block, ("lon", "lat"), route)


def exchange(total, pairs, work=None, args=()):
    sent = total.astype(BF16)
    done = None
    if work is not None:
        sent, args = lax.optimization_barrier((sent, args))
    got = [partner(sent, *pair) for pair in pairs]
    if work is not None:
        got, done = lax.optimization_barrier((got, work(*args)))
    total = sent.astype(F32)
    for other in got:
        total = total + other.astype(F32)
    return total, done


def per_device(input_a, input_b, cot_b, gain, wqkv, wo, pd, pu, od, ou):
    n_lon, n_lat = lax.axis_size("lon"), lax.axis_size("lat")
    polar = (lax.axis_index("lat") == n_lat - 1).astype(jnp.int32).reshape(1)

    x_b, cot, x_a = (jnp.transpose(field, (1, 2, 0, 3)) for field in (input_b, cot_b, input_a))
    below_x, corner, side = run_pack(x_b, cot, x_a)
    below_x, cot_rest, x_a_rest = lax.optimization_barrier((below_x, cot, x_a))
    below_x = shifted(below_x, 0, 1)
    corner = shifted(corner, 1, 1)
    side = shifted(side, 1, 0)
    below_rest = run_pack_rest(cot_rest, x_a_rest)
    below_rest, wqkv, wo = lax.optimization_barrier((below_rest, wqkv, wo))
    below_rest = shifted(below_rest, 0, 1)
    wqkv, wo = run_stage(wqkv, wo)
    weights = (gain.reshape(1, D), wqkv, wo, pd.T, pu, od.T, ou)
    rows_b, *saved = run_encode(polar, x_b, (below_x, corner, side), weights)
    halo = (below_rest, corner, side)
    gp, clq, grads = run_grads(cot, halo, saved, weights)

    core = lax.rem(lax.axis_index("lon"), 2)
    halves = grads[:2], grads[2:]
    kept = jnp.where(core == 0, halves[0], halves[1])
    sent = jnp.where(core == 0, halves[1], halves[0]).astype(BF16)
    total = kept + partner(sent, 1, 0).astype(F32)

    steps = [[(0, 8)], [(0, 1)], [(8, 0)], [(0, 2)], [(0, 4)], [(2, 0)], [(4, 0)]]
    steps = [step for step in steps if all(a < n_lon and b < n_lat for a, b in step)]
    total, (own0_b, below_b, corner_b, own1_b, side_b) = exchange(
        total, steps[0], lambda *a: run_input_grad(*a, weights), (rows_b, gp, clq)
    )
    total, saved = exchange(
        total,
        steps[1],
        lambda *halo: run_forward_first(polar, x_a, halo, weights),
        halo,
    )
    total, (own0_a, below, corner, own1_a, side) = exchange(
        total,
        steps[2],
        lambda *a: run_forward_second(polar, a[:3], a[3:], weights),
        (*saved, below_b, corner_b, side_b),
    )
    below = shifted(below, 0, -1)
    corner = shifted(corner, -1, -1)
    side = shifted(side, -1, 0)
    for step in steps[3:-1]:
        total = exchange(total, step)[0]
    sent = total.astype(BF16)
    outs = run_add(x_a, cot, own0_a, own1_a, own0_b, own1_b, below, corner, side)
    got, output_a, input_grad_b = lax.optimization_barrier((partner(sent, *steps[-1][0]), *outs))
    total = (sent.astype(F32) + got.astype(F32)).astype(BF16)
    other = partner(total, 1, 0)
    output_a, input_grad_b = (jnp.transpose(a, (2, 0, 1, 3)) for a in (output_a, input_grad_b))
    qd, qu, od_grad, ou_grad = run_clip(core.reshape(1), total, other)
    return output_a, input_grad_b, qd.T, qu, od_grad.T, ou_grad


def solution(mesh):
    field = P(None, "lat", "lon", None)
    return jax.shard_map(
        per_device,
        mesh=mesh,
        in_specs=(field,) * 3 + (P(),) * 7,
        out_specs=(field, field, P(), P(), P(), P()),
        check_vma=False,
    )
```

```python
import functools

import jax
import jax.numpy as jnp
from jax import lax
from jax.experimental import pallas as pl
from jax.experimental.pallas import tpu as pltpu
from jax.sharding import PartitionSpec as P

D = 1024
HD = 64
RANK = 8
TOK = 288
WIN = 144
HALF = 72
GH = 4
GW = GH * HD
NG = D // GW
GQ = GH * WIN
EPS = 1e-05
MASKED = -1e30
VMEM = 10 * 1024 * 1024
F32 = jnp.float32
BF16 = jnp.bfloat16


def nn(a, b):
    return jnp.dot(a, b, preferred_element_type=F32)


def nt(a, b):
    return lax.dot_general(a, b, (((1,), (1,)), ((), ())), preferred_element_type=F32)


def tn(a, b):
    return lax.dot_general(a, b, (((0,), (0,)), ((), ())), preferred_element_type=F32)


def layer_norm(tokens):
    average = jnp.mean(tokens, axis=-1, keepdims=True)
    centered = tokens - average
    variance = jnp.mean(centered * centered, axis=-1, keepdims=True)
    inv_std = lax.rsqrt(variance + EPS)
    return centered * inv_std, inv_std


def assemble(pieces, out_ref):
    at = 0
    for piece in pieces:
        rows = piece.shape[-2]
        out_ref[at : at + rows] = piece[...].astype(F32)
        at += rows


def take_apart(rows_ref, pieces):
    at = 0
    for piece in pieces:
        rows = piece.shape[-2]
        piece[...] = rows_ref[at : at + rows].astype(BF16)
        at += rows


def head_lanes(h):
    lane = lax.broadcasted_iota(jnp.int32, (1, GW), 1)
    return (lane >= h * HD) & (lane < (h + 1) * HD)


def spread_heads(a):
    zero = jnp.zeros_like(a)
    return jnp.concatenate([jnp.where(head_lanes(h), a, zero) for h in range(GH)], axis=0)


def gather_heads(a):
    out = a[:WIN]
    for h in range(1, GH):
        out = jnp.where(head_lanes(h), a[h * WIN : (h + 1) * WIN], out)
    return out


def pole_bias(polar):
    key = lax.broadcasted_iota(jnp.int32, (WIN, GQ), 0)
    query = lax.broadcasted_iota(jnp.int32, (WIN, GQ), 1)
    for h in range(1, GH):
        query = jnp.where(query >= WIN, query - WIN, query)
    apart = jnp.not_equal(key < HALF, query < HALF)
    return jnp.where(apart & (polar != 0), MASKED, 0.0)


def softmax_keys(q_blocks, k, bias_ref):
    scores = nt(k, q_blocks) + bias_ref[...]
    top = jnp.max(scores, axis=0, keepdims=True)
    p = jnp.exp(scores - top)
    return p * (1.0 / jnp.sum(p, axis=0, keepdims=True))


def project(normed, low, w_ref, up_ref, cols):
    return (nn(normed, w_ref[:, cols]) + nn(low, up_ref[:, cols])).astype(BF16)


def columns(i, g):
    return slice(i * D + g * GW, i * D + (g + 1) * GW)


def copy_in(pairs, sems):
    copies = [pltpu.make_async_copy(a, b, sems.at[i]) for i, (a, b) in enumerate(pairs)]
    for copy in copies:
        copy.start()
    for copy in copies:
        copy.wait()


def cut_below(rows, out):
    out[:72] = rows[:, :6].reshape(72, D)
    out[72:] = rows[:, 6:].reshape(36, D)


def pack_kernel(x_b, cot, x_a, below, corner, side, upper, *rest):
    firsts, sems = rest[:3], rest[3]
    pairs = [(a.at[:, :3], b) for a, b in zip((x_b, cot, x_a), firsts)]
    copy_in([(x_b.at[:6, 3:], upper), *pairs], sems)
    cut_below(upper, below.at[0])
    for i, first in enumerate(firsts):
        corner[i] = first[:6].reshape(36, D)
        side[i] = first[6:].reshape(36, D)


def pack_rest_kernel(cot, x_a, below, first, second, sems):
    copy_in([(cot.at[:6, 3:], first), (x_a.at[:6, 3:], second)], sems)
    cut_below(first, below.at[0])
    cut_below(second, below.at[1])


def stage_kernel(*refs):
    copy_in(zip(refs[:2], refs[2:4]), refs[4])


def pieces_of(field, below, corner, side):
    own0 = field[6:, 3:9].reshape(72, D)
    own1 = field[6:, 9:].reshape(36, D)
    return own0, below[...], corner[...], own1, side[...]


def attend_group(normed, low, wqkv_ref, pu_ref, bias_ref, g):
    q = project(normed, low, wqkv_ref, pu_ref, columns(0, g)) * 0.125
    k = project(normed, low, wqkv_ref, pu_ref, columns(1, g))
    v = project(normed, low, wqkv_ref, pu_ref, columns(2, g))
    contexts = []
    for w in range(2):
        rows = slice(w * WIN, (w + 1) * WIN)
        weights = softmax_keys(spread_heads(q[rows]), k[rows], bias_ref).astype(BF16)
        contexts.append(gather_heads(tn(weights, v[rows])).astype(BF16))
    return jnp.concatenate(contexts, axis=0)


def forward_first_kernel(
    polar_ref, field, below, corner, side, gain_ref, wqkv_ref, pd_ref, pu_ref,
    normed_ref, low_ref, context_ref, x_ref, bias_ref,
):
    assemble(pieces_of(field, below.at[1], corner.at[2], side.at[2]), x_ref)
    standard, _ = layer_norm(x_ref[...])
    normed = (standard * gain_ref[...]).astype(BF16)
    normed_ref[...] = normed
    low = nt(normed, pd_ref[...]).astype(BF16)
    low_ref[...] = low
    bias_ref[...] = pole_bias(polar_ref[0])
    for g in range(NG // 2):
        context_ref[:, columns(0, g)] = attend_group(normed, low, wqkv_ref, pu_ref, bias_ref, g)


def forward_second_kernel(
    polar_ref, normed_ref, low_ref, context_ref, wqkv_ref, wo_ref, pu_ref, od_ref, ou_ref, below_b,
    corner_b, side_b, own0, below, corner, own1, side, rows_ref, bias_ref,
):
    bias_ref[...] = pole_bias(polar_ref[0])
    normed, low = normed_ref[...], low_ref[...]
    groups = [
        attend_group(normed, low, wqkv_ref, pu_ref, bias_ref, g) for g in range(NG // 2, NG)
    ]
    context = jnp.concatenate([context_ref[...], *groups], axis=1)
    low_out = nt(context, od_ref[...]).astype(BF16)
    rows_ref[...] = nn(context, wo_ref[...]) + nn(low_out, ou_ref[...])
    take_apart(rows_ref, [a.at[0] for a in (own0, below, corner, own1, side)])
    below[1] = below_b[...]
    corner[1] = corner_b[...]
    side[1] = side_b[...]


def encode_kernel(
    polar_ref, field, below, corner, side, gain_ref, wqkv_ref, pd_ref, pu_ref, od_ref,
    x_ref, normed_ref, lowt_ref, qkv_ref, soft_ref, context_ref, lowt_out_ref, bias_ref,
):
    assemble(pieces_of(field, below.at[0], corner.at[0], side.at[0]), x_ref)
    standard, _ = layer_norm(x_ref[...])
    normed = (standard * gain_ref[...]).astype(BF16)
    normed_ref[...] = normed
    low = nt(normed, pd_ref[...])
    lowt_ref[...] = low.T.astype(BF16)
    low = low.astype(BF16)
    bias_ref[...] = pole_bias(polar_ref[0])
    low_out = jnp.zeros((TOK, RANK), F32)
    for g in range(NG):
        q = project(normed, low, wqkv_ref, pu_ref, columns(0, g)) * 0.125
        k = project(normed, low, wqkv_ref, pu_ref, columns(1, g))
        v = project(normed, low, wqkv_ref, pu_ref, columns(2, g))
        for i, a in enumerate((q, k, v)):
            qkv_ref[:, columns(i, g)] = a
        contexts = []
        for w in range(2):
            rows = slice(w * WIN, (w + 1) * WIN)
            softmaxed = softmax_keys(spread_heads(q[rows]), k[rows], bias_ref)
            soft_ref[2 * g + w] = softmaxed
            contexts.append(gather_heads(tn(softmaxed.astype(BF16), v[rows])).astype(BF16))
        context = jnp.concatenate(contexts, axis=0)
        context_ref[:, columns(0, g)] = context
        low_out += nt(context, od_ref[:, columns(0, g)])
    lowt_out_ref[...] = low_out.T.astype(BF16)


def grads_kernel(
    field, below, corner, side, normed_ref, lowt_ref, qkv_ref, soft_ref, context_ref, lowt_out_ref,
    wo_ref, pu_ref, od_ref, ou_ref, gp_ref, clq_ref, grads_ref, rows_ref,
):
    assemble(pieces_of(field, below.at[0], corner.at[1], side.at[1]), rows_ref)
    cot = rows_ref[...].astype(BF16)
    clo = nt(cot, ou_ref[...])
    clot = clo.T.astype(BF16)
    clo = clo.astype(BF16)
    lowt = lowt_ref[...]
    cl = jnp.zeros((TOK, RANK), F32)
    for g in range(NG):
        own = columns(0, g)
        q, k, v = (qkv_ref[:, columns(i, g)] for i in range(3))
        grad_context = (nt(cot, wo_ref[own, :]) + nn(clo, od_ref[:, own])).astype(BF16)
        gqs, gks, gvs = [], [], []
        for w in range(2):
            rows = slice(w * WIN, (w + 1) * WIN)
            q_blocks, g_blocks = spread_heads(q[rows]), spread_heads(grad_context[rows])
            softmaxed = soft_ref[2 * g + w]
            grad_weights = nt(v[rows], g_blocks)
            inner = jnp.sum(grad_weights * softmaxed, axis=0, keepdims=True)
            grad_scores = (softmaxed * (grad_weights - inner)).astype(BF16)
            gqs.append((gather_heads(tn(grad_scores, k[rows])) * 0.125).astype(BF16))
            gks.append(nn(grad_scores, q_blocks).astype(BF16))
            gvs.append(nn(softmaxed.astype(BF16), g_blocks).astype(BF16))
        for i, parts in enumerate((gqs, gks, gvs)):
            gp = jnp.concatenate(parts, axis=0)
            gp_ref[:, columns(i, g)] = gp
            grads_ref[g, 8 * i : 8 * i + 8] = nn(lowt, gp)
            cl += nt(gp, pu_ref[:, columns(i, g)])
        grads_ref[g, 24:32] = nn(clot, context_ref[:, own])
    clq_ref[...] = cl.astype(BF16)
    down = nn(cl.T.astype(BF16), normed_ref[...])
    up = nn(lowt_out_ref[...], cot)
    for g in range(NG):
        grads_ref[g, 32:40] = down[:, g * GW : (g + 1) * GW]
        grads_ref[g, 40:48] = up[:, g * GW : (g + 1) * GW]


def input_grad_kernel(
    x_ref, gain_ref, gp_ref, wqkv_ref, clq_ref, pd_ref, o0, o1, o2, o3, o4, rows_ref
):
    standard, inv_std = layer_norm(x_ref[...])
    grad_normed = nt(gp_ref[...], wqkv_ref[...]) + nn(clq_ref[...], pd_ref[...])
    grad_hat = grad_normed * gain_ref[...]
    along = jnp.mean(grad_hat * standard, axis=-1, keepdims=True)
    mean = jnp.mean(grad_hat, axis=-1, keepdims=True)
    rows_ref[...] = inv_std * (grad_hat - mean - standard * along)
    take_apart(rows_ref, (o0, o1, o2, o3, o4))


def add_kernel(field_a, field_b, own0_a, own1_a, own0_b, own1_b, below, corner, side, out_a, out_b):
    parts = ((field_a, own0_a.at[0], own1_a.at[0], out_a), (field_b, own0_b, own1_b, out_b))
    for i, (field, own0, own1, out) in enumerate(parts):
        places = (
            (slice(0, 6), slice(0, 3), corner[i]),
            (slice(0, 6), slice(3, 9), below[i, :72]),
            (slice(0, 6), slice(9, 12), below[i, 72:]),
            (slice(6, 12), slice(0, 3), side[i]),
            (slice(6, 12), slice(3, 9), own0[...]),
            (slice(6, 12), slice(9, 12), own1[...]),
        )
        for rows, cols, piece in places:
            here = field[rows, cols]
            out[rows, cols] = (here.astype(F32) + piece.reshape(here.shape).astype(F32)).astype(BF16)


def clip_kernel(first_ref, mine_ref, other_ref, qd_ref, qu_ref, od_ref, ou_ref):
    mine, other = mine_ref[...].astype(F32), other_ref[...].astype(F32)
    total = jnp.sum(jnp.sum(mine * mine, axis=(0, 1)) + jnp.sum(other * other, axis=(0, 1)))
    limit = jnp.sqrt(jnp.full((8, GW), 6.0 * D * RANK, F32))
    factor = jnp.minimum(1.0, limit / (jnp.sqrt(jnp.full((8, GW), total)) + 1e-06))
    is_first = first_ref[0] == 0
    for g in range(NG):
        own = mine[g % 2]
        far = other[g % 2]
        part = jnp.where(is_first, own, far) if g < 2 else jnp.where(is_first, far, own)
        cols = slice(g * GW, (g + 1) * GW)
        for i in range(3):
            qu_ref[:, columns(i, g)] = part[8 * i : 8 * i + 8] * factor
        od_ref[:, cols] = part[24:32] * factor
        qd_ref[:, cols] = part[32:40] * factor
        ou_ref[:, cols] = part[40:48] * factor


SMEM_SPEC = pl.BlockSpec(memory_space=pltpu.SMEM)
VMEM_SPEC = pl.BlockSpec(memory_space=pltpu.VMEM)
PIECES = (72, 108, 36, 36, 36)


def cost(us):
    return pl.CostEstimate(flops=us * 1000000000, bytes_accessed=4000000, transcendentals=0)


def call(kernel, name, us, scalars, arrays, outs, scratch):
    return pl.pallas_call(
        kernel,
        in_specs=[SMEM_SPEC] * len(scalars) + [VMEM_SPEC] * len(arrays),
        out_specs=[VMEM_SPEC] * len(outs),
        out_shape=[jax.ShapeDtypeStruct(shape, dtype) for shape, dtype in outs],
        scratch_shapes=scratch,
        compiler_params=pltpu.CompilerParams(vmem_limit_bytes=VMEM),
        cost_estimate=cost(us),
        name=name,
    )(*scalars, *arrays)


PIECE_OUTS = [((rows, D), BF16) for rows in PIECES]
ROWS_SCRATCH = pltpu.VMEM((TOK, D), F32)
BIAS_SCRATCH = pltpu.VMEM((WIN, GQ), F32)


def call_far(kernel, name, us, arrays, outs, buffers, copies):
    return pl.pallas_call(
        kernel,
        in_specs=[pl.BlockSpec(memory_space=pltpu.HBM)] * len(arrays),
        out_specs=[VMEM_SPEC] * len(outs),
        out_shape=[jax.ShapeDtypeStruct(shape, BF16) for shape in outs],
        scratch_shapes=[
            *[pltpu.VMEM(shape, BF16) for shape in buffers],
            pltpu.SemaphoreType.DMA((copies,)),
        ],
        compiler_params=pltpu.CompilerParams(vmem_limit_bytes=VMEM),
        cost_estimate=cost(us),
        name=name,
    )(*[pltpu.with_memory_space_constraint(a, pltpu.HBM) for a in arrays])


def run_pack(x_b, cot, x_a):
    outs = [(1, 108, D), (3, 36, D), (3, 36, D)]
    buffers = [(6, 9, 2, D)] + [(12, 3, 2, D)] * 3
    return call_far(pack_kernel, "pack", 20, [x_b, cot, x_a], outs, buffers, 4)


def run_pack_rest(cot, x_a):
    return call_far(pack_rest_kernel, "pack_rest", 2, [cot, x_a], [(2, 108, D)], [(6, 9, 2, D)] * 2, 2)[0]


def run_stage(wqkv, wo):
    return call_far(stage_kernel, "stage", 3, [wqkv, wo], [wqkv.shape, wo.shape], [], 2)


def run_forward_first(polar, field, halo, weights):
    gain, wqkv, _, pd, pu, _, _ = weights
    outs = [((TOK, D), BF16), ((TOK, RANK), BF16), ((TOK, D // 2), BF16)]
    arrays = [field, *halo, gain, wqkv, pd, pu]
    scratch = [ROWS_SCRATCH, BIAS_SCRATCH]
    return call(forward_first_kernel, "forward_first", 4, [polar], arrays, outs, scratch)


def run_forward_second(polar, saved, pieces_b, weights):
    _, wqkv, wo, _, pu, od, ou = weights
    outs = [((n, rows, D), BF16) for n, rows in ((1, 72), (2, 108), (2, 36), (1, 36), (2, 36))]
    arrays = [*saved, wqkv, wo, pu, od, ou, *pieces_b]
    scratch = [ROWS_SCRATCH, BIAS_SCRATCH]
    return call(forward_second_kernel, "forward_second", 4, [polar], arrays, outs, scratch)


def run_encode(polar, field, halo, weights):
    gain, wqkv, _, pd, pu, od, _ = weights
    outs = [
        ((TOK, D), F32),
        ((TOK, D), BF16),
        ((RANK, TOK), BF16),
        ((TOK, 3 * D), BF16),
        ((2 * NG, WIN, GQ), F32),
        ((TOK, D), BF16),
        ((RANK, TOK), BF16),
    ]
    arrays = [field, *halo, gain, wqkv, pd, pu, od]
    return call(encode_kernel, "encode", 7, [polar], arrays, outs, [BIAS_SCRATCH])


def run_grads(field, halo, saved, weights):
    _, _, wo, _, pu, od, ou = weights
    outs = [((TOK, 3 * D), BF16), ((TOK, RANK), BF16), ((NG, 48, GW), F32)]
    arrays = [field, *halo, *saved, wo, pu, od, ou]
    return call(grads_kernel, "grads", 7, [], arrays, outs, [ROWS_SCRATCH])


def run_input_grad(x, gp, clq, weights):
    gain, wqkv, _, pd, _, _, _ = weights
    return call(
        input_grad_kernel, "input_grad", 3, [], [x, gain, gp, wqkv, clq, pd], PIECE_OUTS, [ROWS_SCRATCH]
    )


def run_add(*arrays):
    return call(add_kernel, "add", 3, [], arrays, [((12, 12, 2, D), BF16)] * 2, [])


def run_clip(first, mine, other):
    outs = [((RANK, n), F32) for n in (D, 3 * D, D, D)]
    return call(clip_kernel, "clip", 1, [first], [mine, other], outs, [])


def shifted(block, lon, lat):
    n_lon, n_lat = lax.axis_size("lon"), lax.axis_size("lat")
    route = [
        (((i + lon) % n_lon) * n_lat + (j + lat) % n_lat, i * n_lat + j)
        for i in range(n_lon)
        for j in range(n_lat)
    ]
    return lax.ppermute(block, ("lon", "lat"), route)


def partner(block, lon_bit, lat_bit):
    n_lon, n_lat = lax.axis_size("lon"), lax.axis_size("lat")
    route = [
        ((i ^ lon_bit) * n_lat + (j ^ lat_bit), i * n_lat + j) for i in range(n_lon) for j in range(n_lat)
    ]
    return lax.ppermute(block, ("lon", "lat"), route)


def exchange(total, pairs, work=None, args=()):
    sent = total.astype(BF16)
    done = None
    if work is not None:
        sent, args = lax.optimization_barrier((sent, args))
    got = [partner(sent, *pair) for pair in pairs]
    if work is not None:
        got, done = lax.optimization_barrier((got, work(*args)))
    total = sent.astype(F32)
    for other in got:
        total = total + other.astype(F32)
    return total, done


def per_device(input_a, input_b, cot_b, gain, wqkv, wo, pd, pu, od, ou):
    n_lon, n_lat = lax.axis_size("lon"), lax.axis_size("lat")
    polar = (lax.axis_index("lat") == n_lat - 1).astype(jnp.int32).reshape(1)

    x_b, cot, x_a = (jnp.transpose(field, (1, 2, 0, 3)) for field in (input_b, cot_b, input_a))
    below_x, corner, side = run_pack(x_b, cot, x_a)
    below_x, cot_rest, x_a_rest = lax.optimization_barrier((below_x, cot, x_a))
    below_x = shifted(below_x, 0, 1)
    corner = shifted(corner, 1, 1)
    side = shifted(side, 1, 0)
    below_rest = run_pack_rest(cot_rest, x_a_rest)
    below_rest, wqkv, wo = lax.optimization_barrier((below_rest, wqkv, wo))
    below_rest = shifted(below_rest, 0, 1)
    wqkv, wo = run_stage(wqkv, wo)
    weights = (gain.reshape(1, D), wqkv, wo, pd.T, pu, od.T, ou)
    rows_b, *saved = run_encode(polar, x_b, (below_x, corner, side), weights)
    halo = (below_rest, corner, side)
    gp, clq, grads = run_grads(cot, halo, saved, weights)

    core = lax.rem(lax.axis_index("lon"), 2)
    halves = grads[:2], grads[2:]
    kept = jnp.where(core == 0, halves[0], halves[1])
    sent = jnp.where(core == 0, halves[1], halves[0]).astype(BF16)
    total = kept + partner(sent, 1, 0).astype(F32)

    steps = [[(0, 8)], [(0, 1), (8, 0), (8, 1)], [(0, 2)], [(0, 4)], [(2, 0)], [(4, 0)]]
    steps = [step for step in steps if all(a < n_lon and b < n_lat for a, b in step)]
    def far_step(rows_b, gp, clq, *halo):
        return run_input_grad(rows_b, gp, clq, weights), run_forward_first(polar, x_a, halo, weights)

    total, (pieces_b, saved) = exchange(total, steps[0], far_step, (rows_b, gp, clq, *halo))
    own0_b, below_b, corner_b, own1_b, side_b = pieces_b
    total, (own0_a, below, corner, own1_a, side) = exchange(
        total,
        steps[1],
        lambda *a: run_forward_second(polar, a[:3], a[3:], weights),
        (*saved, below_b, corner_b, side_b),
    )
    below = shifted(below, 0, -1)
    corner = shifted(corner, -1, -1)
    side = shifted(side, -1, 0)
    for step in steps[2:-1]:
        total = exchange(total, step)[0]
    sent = total.astype(BF16)
    outs = run_add(x_a, cot, own0_a, own1_a, own0_b, own1_b, below, corner, side)
    got, output_a, input_grad_b = lax.optimization_barrier((partner(sent, *steps[-1][0]), *outs))
    total = (sent.astype(F32) + got.astype(F32)).astype(BF16)
    other = partner(total, 1, 0)
    output_a, input_grad_b = (jnp.transpose(a, (2, 0, 1, 3)) for a in (output_a, input_grad_b))
    qd, qu, od_grad, ou_grad = run_clip(core.reshape(1), total, other)
    return output_a, input_grad_b, qd.T, qu, od_grad.T, ou_grad


def solution(mesh):
    field = P(None, "lat", "lon", None)
    return jax.shard_map(
        per_device,
        mesh=mesh,
        in_specs=(field,) * 3 + (P(),) * 7,
        out_specs=(field, field, P(), P(), P(), P()),
        check_vma=False,
    )
```
